32 devices in a mesh: band: 8 (over z, x), lev: 4 (over y, core).
Axes of the slice: x: 2, y: 2, z: 4, core: 2. Of those that a mesh axis runs over, the one named last changes fastest.
Arguments:
- temp_spectrum: bfloat16 [160, 1280, 2, 136], P('band', None, None, 'lev'), may hold values from -0.875 to 0.875
- surf_spectrum: bfloat16 [160, 1280, 2], P('band'), may hold values from -0.875 to 0.875
- legendre: bfloat16 [160, 16, 1280], P('band'), may hold values from -0.15625 to 0.15625
- m_order: int32 [160], replicated, may hold values from 0 to 159, each once
- hydro_matrix: bfloat16 [136, 136], P('lev'), may hold values from 0.029907227 to 0.29882812
- surf_coupling: float32 [136], P('lev'), may hold values from 0.3 to 3
- src_blocks: int32 [640, 4], P('band'), may hold values from 0 to 639, as said below
- tap_index: int32 [640, 4, 128], P('band'), may hold values from 0 to 511
- tap_weight: float32 [640, 4, 128], P('band'), may hold values from 0.05 to 0.45
Outputs:
- departed: float32 [16, 136, 5120], P('band', 'lev')
The draws below stay inside these ranges and needn't reach their ends.
Inputs may be any that keep to these rules, and one draw needn't show every extreme that they name: `src_blocks`: slots 0 and 2 of a reader block name blocks of the reader's own band device, slot 1 a block of the device before it and slot 3 a block of the device after it, or of the reader's own device where that neighbour does not exist. The readers of one device name at most 16 distinct blocks of each neighbour, and some device names exactly 16 of one neighbour.
All inputs are finite; a program needn't handle non-finite values.
Results may differ from the reference program's by a relative error of at most 0.0047.
Values may be sent and summed in bfloat16 or wider, within the bound.
A program may use at most 128 MiB of HBM per device.

```python
import math
import jax
import jax.numpy as jnp
from jax import lax

NN = 1280
LEV = 136
NLON = 5120
BLK = 128
SLOTS = 4
TAPS = 4
CAP = 16
LAT_DEV = 2
MM = 160
LAT = 16
NB = 640


def draw_src_blocks(key, part):
    per_device = LAT_DEV * NLON // BLK
    band_count = NB // per_device
    key_list = jax.random.split(key, 4)
    reader = jnp.arange(NB, dtype=jnp.int32)
    device_of = reader // per_device
    local_idx = reader % per_device
    own_first = device_of * per_device + jax.random.randint(key_list[0], (NB,), 0, per_device)
    own_second = device_of * per_device + jax.random.randint(key_list[1], (NB,), 0, per_device)

    def one_side(side_key, offset):
        key_counts, key_forced, key_order, key_spare = jax.random.split(side_key, 4)
        counts = jax.random.randint(key_counts, (band_count,), max(1, CAP // 4), CAP + 1)
        forced = jax.random.randint(key_forced, (), 0, band_count - 1)
        forced_device = jnp.where(offset < 0, forced + 1, forced)
        counts = counts.at[forced_device].set(CAP)
        orderings = jax.vmap(lambda sub_key: jax.random.permutation(sub_key, per_device))(jax.random.split(key_order, band_count))
        neighbour = device_of + offset
        exists = (neighbour >= 0) & (neighbour < band_count)
        chosen = orderings[device_of, local_idx % counts[device_of]].astype(jnp.int32)
        spare = device_of * per_device + jax.random.randint(key_spare, (NB,), 0, per_device)
        return jnp.where(exists, neighbour * per_device + chosen, spare).astype(jnp.int32)
    from_before = one_side(key_list[2], -1)
    from_after = one_side(key_list[3], 1)
    return jnp.stack([own_first, from_before, own_second, from_after], axis=1).astype(jnp.int32)


def plant(entries, own_key, low, high):
    spot = [jax.random.randint(jax.random.fold_in(own_key, axis), (), 0, length) for axis, length in enumerate(entries.shape)]
    longest = entries.shape.index(max(entries.shape))
    beside = spot[:longest] + [(spot[longest] + 1) % entries.shape[longest]] + spot[longest + 1:]
    return entries.at[tuple(spot)].set(low).at[tuple(beside)].set(high)


def levels(stream_key, extent, shards, smallest, high):
    gain = 1.0
    for position, parts in shards:
        heights = jax.random.uniform(jax.random.fold_in(jax.random.fold_in(stream_key, 6), position), (parts,), jnp.float32, smallest / len(shards), high / len(shards))
        gain = gain * jnp.repeat(jnp.exp(heights), extent[position] // parts).reshape((-1,) + (1,) * (len(extent) - 1 - position))
    return gain


def noise(stream_key, extent, width, bound, pieces=(), kind=jnp.bfloat16):
    array = width * jax.random.normal(stream_key, extent, jnp.float32)
    if pieces:
        array = array * levels(stream_key, extent, pieces, -0.22, 0.18)
    return jnp.clip(array, -bound, bound).astype(kind)


def setup_inputs(seed: int = 0) -> dict:
    arg_keys = jax.random.split(jax.random.key(seed), 10)
    return {
        "temp_spectrum": noise(arg_keys[0], (MM, NN, 2, LEV), ((2 * MM) ** -0.5), 0.875, ((0, 8), (3, 4))),
        "surf_spectrum": noise(arg_keys[1], (MM, NN, 2), ((2 * MM) ** -0.5), 0.875, ((0, 8),)),
        "legendre": noise(arg_keys[2], (MM, LAT, NN), NN ** -0.5, 0.15625, ((0, 8),)),
        "m_order": jax.random.permutation(arg_keys[3], MM).astype(jnp.int32),
        "hydro_matrix": jnp.clip(jnp.exp(math.log(0.29882812) - 2.30176843 * jax.random.uniform(arg_keys[4], (LEV, LEV), jnp.float32) ** levels(arg_keys[4], (LEV, LEV), ((0, 4),), -0.2, 0.2)), 0.029907227, 0.29882812).astype(jnp.bfloat16),
        "surf_coupling": jnp.clip(jnp.exp(math.log(3.0) - 2.3025851 * jax.random.uniform(arg_keys[5], (LEV,), jnp.float32) ** levels(arg_keys[5], (LEV,), ((0, 4),), -0.2, 0.2)), 0.3, 3.0),
        "src_blocks": draw_src_blocks(jax.random.fold_in(arg_keys[9], 71), 0),
        "tap_index": plant(jax.random.randint(arg_keys[7], (NB, TAPS, BLK), 0, SLOTS * BLK), jax.random.fold_in(arg_keys[7], 1), 0, (SLOTS * BLK) - 1).astype(jnp.int32),
        "tap_weight": jnp.clip(0.05 + 0.39999999 * jax.random.uniform(arg_keys[8], (NB, TAPS, BLK), jnp.float32) ** levels(arg_keys[8], (NB, TAPS, BLK), ((0, 8),), -0.2, 0.2), 0.05, 0.45),
    }


def synth_table(m_values, nlon):
    columns = lax.broadcasted_iota(jnp.int32, (m_values.shape[0], nlon), 1)
    phase = (m_values[:, None] * columns) % nlon
    angle = phase.astype(jnp.float32) * (2.0 * math.pi / nlon)
    factor = jnp.where(m_values == 0, 1.0, 2.0).astype(jnp.float32)[:, None]
    return jnp.stack([factor * jnp.cos(angle), -factor * jnp.sin(angle)], axis=1).astype(jnp.bfloat16)


def reference(temp_spectrum, surf_spectrum, legendre, m_order, hydro_matrix, surf_coupling, src_blocks, tap_index, tap_weight):
    n_index = jnp.arange(NN, dtype=jnp.int32)
    keep = n_index[None, :] >= m_order[:, None]
    masked_t = jnp.where(keep[:, :, None, None], temp_spectrum, jnp.zeros_like(temp_spectrum))
    masked_p = jnp.where(keep[:, :, None], surf_spectrum, jnp.zeros_like(surf_spectrum))
    joined = jnp.concatenate([masked_t.reshape(MM, NN, 2 * LEV), masked_p], axis=2)

    def legendre_slot(pair):
        values, coeffs = pair
        return jnp.dot(values, coeffs, preferred_element_type=jnp.float32).astype(jnp.bfloat16)

    four = lax.map(legendre_slot, (legendre, joined))
    four_t = four[:, :, :2 * LEV].reshape(MM, LAT, 2, LEV)
    four_p = four[:, :, 2 * LEV:]
    table = synth_table(m_order, NLON).reshape(MM * 2, NLON)
    rows = lax.broadcasted_iota(jnp.int32, (LEV, LEV), 0)
    cols = lax.broadcasted_iota(jnp.int32, (LEV, LEV), 1)
    hmat = jnp.where(cols >= rows, hydro_matrix, jnp.zeros_like(hydro_matrix)).astype(jnp.float32)

    def per_latitude(pair):
        coeff_t, coeff_p = pair
        temp_grid = jnp.dot(coeff_t.reshape(MM * 2, LEV).T, table, preferred_element_type=jnp.float32)
        surf_grid = jnp.dot(coeff_p.reshape(1, MM * 2), table, preferred_element_type=jnp.float32)[0]
        geopot = jnp.dot(hmat, temp_grid, precision=lax.Precision.HIGHEST) + surf_coupling[:, None] * surf_grid[None, :]
        return geopot.astype(jnp.bfloat16)

    geopot = lax.map(per_latitude, (jnp.moveaxis(four_t, 1, 0), jnp.moveaxis(four_p, 1, 0)))
    pool = jnp.transpose(geopot, (1, 0, 2)).reshape(LEV, LAT * NLON)
    slot_of = tap_index // BLK
    cell = tap_index % BLK
    block = jnp.take_along_axis(src_blocks, slot_of.reshape(NB, TAPS * BLK), axis=1).reshape(NB, TAPS, BLK)
    flat = block * BLK + cell

    def per_level(level_row):
        values = level_row[flat].astype(jnp.float32)
        return jnp.sum(values * tap_weight, axis=1)

    moved = lax.map(per_level, pool)
    return jnp.transpose(moved.reshape(LEV, LAT, NLON), (1, 0, 2))
```

```python
import functools
import math

import jax
import jax.numpy as jnp
from jax import lax
from jax.experimental import pallas as pl
from jax.experimental.pallas import tpu as pltpu
from jax.sharding import PartitionSpec as P

NLON = 5120
BLK = 128
SLOTS = 4
TAPS = 4
XB = NLON // BLK
SP = 24
RS = 2 * SP
LR = 48
KP = 40
JJ = 6
WIDE = 256
MESH = pl.DeviceIdType.MESH


def exchange_kernel(nb, nl, f_ref, h_ref, out_ref, fall, ft, pieces, sa, ra, sb, rb):
    band = lax.axis_index("band")
    lev = lax.axis_index("lev")
    barrier = pltpu.get_barrier_semaphore()

    def greet_lev(i, _):
        pl.semaphore_signal(
            barrier, inc=1, device_id=(band, lax.rem(lev + i, nl)), device_id_type=MESH
        )
        return 0

    def greet_band(i, _):
        pl.semaphore_signal(
            barrier, inc=1, device_id=(lax.rem(band + i, nb), lev), device_id_type=MESH
        )
        return 0

    lax.fori_loop(1, nl, greet_lev, 0)
    lax.fori_loop(1, nb, greet_band, 0)
    pl.semaphore_wait(barrier, nl - 1 + nb - 1)

    def copy_a(i):
        peer = lax.rem(lev + i, nl)
        return pltpu.make_async_remote_copy(
            src_ref=f_ref,
            dst_ref=fall.at[lev],
            send_sem=sa.at[i],
            recv_sem=ra.at[i],
            device_id=(band, peer),
            device_id_type=MESH,
        )

    for i in range(1, nl):
        copy_a(i).start()
    width = f_ref.shape[1]
    edge = 2 * RS
    zero = jnp.zeros((edge, nl * LR), jnp.bfloat16)
    ft[0:edge, :] = zero
    ft[edge + width : edge + width + edge, :] = zero
    fall[lev] = f_ref[...]
    for i in range(1, nl):
        copy_a(i).wait()
    step = 768
    for c in range(0, width, step):
        part = fall[:, :, c : c + step].reshape(nl * LR, step).astype(jnp.float32)
        ft[edge + c : edge + c + step, :] = part.T.astype(jnp.bfloat16)
    h = h_ref[...]

    def make(b, _):
        total = jnp.zeros((RS, WIDE), jnp.float32)
        for jj in range(JJ):
            rows = ft[pl.ds(pl.multiple_of((2 * b + jj) * RS, 16), RS), :]
            total = total + jnp.dot(rows, h[jj], preferred_element_type=jnp.float32)
        pieces[b] = total.astype(jnp.bfloat16)
        return 0

    lax.fori_loop(0, nb, make, 0)

    def copy_b(i):
        peer = lax.rem(band + i, nb)
        return pltpu.make_async_remote_copy(
            src_ref=pieces.at[peer],
            dst_ref=out_ref.at[band],
            send_sem=sb.at[i],
            recv_sem=rb.at[i],
            device_id=(peer, lev),
            device_id_type=MESH,
        )

    def send(i, _):
        copy_b(i).start()
        return 0

    lax.fori_loop(1, nb, send, 0)
    out_ref[band] = pieces[band]

    def done(i, _):
        copy_b(i).wait()
        return 0

    lax.fori_loop(1, nb, done, 0)


def exchange(f, h, nb, nl):
    width = f.shape[1]
    vmem = pl.BlockSpec(memory_space=pltpu.VMEM)
    return pl.pallas_call(
        functools.partial(exchange_kernel, nb, nl),
        out_shape=jax.ShapeDtypeStruct((nb, RS, WIDE), jnp.bfloat16),
        in_specs=[vmem, vmem],
        out_specs=vmem,
        scratch_shapes=[
            pltpu.VMEM((nl, LR, width), jnp.bfloat16),
            pltpu.VMEM((width + 4 * RS, nl * LR), jnp.bfloat16),
            pltpu.VMEM((nb, RS, WIDE), jnp.bfloat16),
            pltpu.SemaphoreType.DMA((nl,)),
            pltpu.SemaphoreType.DMA((nl,)),
            pltpu.SemaphoreType.DMA((nb,)),
            pltpu.SemaphoreType.DMA((nb,)),
        ],
        compiler_params=pltpu.CompilerParams(
            collective_id=0, has_side_effects=True, vmem_limit_bytes=41943040
        ),
    )(f, h)


def grid_kernel(nb, lev_dev, src_ref, coef_ref, wave_ref, idx_ref, wgt_ref, out_ref, table, pool):
    def build(b, _):
        rows = pl.ds(pl.multiple_of(b * SP, 8), SP)
        real, imag = wave_ref[0, rows, :], wave_ref[1, rows, :]
        turn_c, turn_s = wave_ref[2, rows, :], wave_ref[3, rows, :]
        place = pl.ds(pl.multiple_of(b * RS, 16), RS)
        for x in range(XB):
            both = jnp.concatenate([real, -imag], axis=0)
            table[place, x * BLK : (x + 1) * BLK] = both.astype(jnp.bfloat16)
            real, imag = real * turn_c - imag * turn_s, imag * turn_c + real * turn_s
        return 0

    lax.fori_loop(0, nb, build, 0)
    coef = coef_ref[...].reshape(nb * RS, WIDE).astype(jnp.float32).T.astype(jnp.bfloat16)
    group = 4

    def synth(c, _):
        cols = pl.ds(pl.multiple_of(c * (group * BLK), 128), group * BLK)
        grid = jnp.dot(coef, table[:, cols], preferred_element_type=jnp.float32)
        for jj in range(JJ):
            for g in range(group):
                pool[jj * XB + c * group + g] = grid[
                    jj * KP : (jj + 1) * KP, g * BLK : (g + 1) * BLK
                ]
        return 0

    lax.fori_loop(0, XB // group, synth, 0)
    half = 2 * BLK
    cells = lax.broadcasted_iota(jnp.int32, (half, BLK), 0).astype(jnp.bfloat16)
    zero = jnp.zeros((half, BLK), jnp.bfloat16)

    def read(b):
        idx = idx_ref[b]
        wgt = wgt_ref[b].astype(jnp.bfloat16)
        total = None
        for h in range(2):
            spot = (idx - h * half).astype(jnp.float32).astype(jnp.bfloat16)
            spread = zero
            for t in range(TAPS):
                hit = cells == jnp.broadcast_to(spot[t : t + 1, :], (half, BLK))
                spread = spread + jnp.where(
                    hit, jnp.broadcast_to(wgt[t : t + 1, :], (half, BLK)), zero
                )
            source = jnp.concatenate(
                [pool[src_ref[b, 2 * h]], pool[src_ref[b, 2 * h + 1]]], axis=1
            ).astype(jnp.bfloat16)
            part = jnp.dot(source, spread, preferred_element_type=jnp.float32)
            total = part if total is None else total + part
        return total

    for j in range(2):

        def step(x, _):
            for u in range(2):
                xb = x * 2 + u
                out_ref[j, :, pl.ds(pl.multiple_of(xb * BLK, 128), BLK)] = read(j * XB + xb)[
                    :lev_dev
                ]
            return 0

        lax.fori_loop(0, XB // 2, step, 0)


def grid_part(src, coef, wave, idx, wgt, nb, lev_dev):
    vmem = pl.BlockSpec(memory_space=pltpu.VMEM)
    return pl.pallas_call(
        functools.partial(grid_kernel, nb, lev_dev),
        out_shape=jax.ShapeDtypeStruct((2, lev_dev, NLON), jnp.float32),
        in_specs=[pl.BlockSpec(memory_space=pltpu.SMEM)] + [vmem] * 4,
        out_specs=vmem,
        scratch_shapes=[
            pltpu.VMEM((nb * RS, NLON), jnp.bfloat16),
            pltpu.VMEM((JJ * XB, KP, BLK), jnp.float32),
        ],
        compiler_params=pltpu.CompilerParams(vmem_limit_bytes=58720256),
    )(src, coef, wave, idx, wgt)


def waves(m_order, nb, slots):
    orders = jnp.pad(m_order.reshape(nb, slots), ((0, 0), (0, SP - slots)), constant_values=-1)
    orders = orders.reshape(nb * SP)[:, None]
    points = lax.broadcasted_iota(jnp.int32, (nb * SP, BLK), 1)
    scale = 2.0 * math.pi / NLON
    start = (orders * points % NLON).astype(jnp.float32) * scale
    turn = jnp.broadcast_to(orders * BLK % NLON, points.shape).astype(jnp.float32) * scale
    factor = jnp.where(orders < 0, 0.0, jnp.where(orders == 0, 1.0, 2.0)).astype(jnp.float32)
    return jnp.stack(
        [factor * jnp.cos(start), factor * jnp.sin(start), jnp.cos(turn), jnp.sin(turn)]
    )


def shards(
    temp_spectrum,
    surf_spectrum,
    legendre,
    m_order,
    hydro_matrix,
    surf_coupling,
    src_blocks,
    tap_index,
    tap_weight,
):
    slots, n_count, _, lev_dev = temp_spectrum.shape
    lat_all = legendre.shape[1]
    nb, nl = lax.axis_size("band"), lax.axis_size("lev")
    band, lev = lax.axis_index("band"), lax.axis_index("lev")
    my_orders = lax.dynamic_slice_in_dim(m_order, band * slots, slots)
    n_index = jnp.arange(n_count, dtype=jnp.int32)
    keep = n_index[None, None, :] >= my_orders[:, None, None]
    values = jnp.where(keep, legendre, jnp.zeros_like(legendre))
    four_t = jnp.einsum(
        "sjn,snrk->sjrk", values, temp_spectrum, preferred_element_type=jnp.float32
    ).astype(jnp.bfloat16)
    four_p = jnp.einsum(
        "sjn,snr->sjr", values, surf_spectrum, preferred_element_type=jnp.float32
    ).astype(jnp.bfloat16)
    four = jnp.concatenate([four_t, four_p[..., None]], axis=3)
    four = jnp.transpose(four, (3, 1, 2, 0))
    four = jnp.pad(four, ((0, LR - lev_dev - 1), (0, 0), (0, 0), (0, SP - slots)))
    four = four.reshape(LR, lat_all * RS)

    lev_total = hydro_matrix.shape[1]
    rows = lax.broadcasted_iota(jnp.int32, (lev_dev, lev_total), 0) + lev * lev_dev
    cols = lax.broadcasted_iota(jnp.int32, (lev_dev, lev_total), 1)
    hmat = jnp.where(cols >= rows, hydro_matrix, jnp.zeros_like(hydro_matrix))
    hmat = hmat.reshape(lev_dev, nl, lev_dev)
    surf = jnp.where(jnp.arange(nl)[None, :] == lev, surf_coupling[:, None], 0.0)
    hmat = jnp.concatenate([hmat, surf.astype(jnp.bfloat16)[:, :, None]], axis=2)
    hmat = jnp.pad(hmat, ((0, KP - lev_dev), (0, 0), (0, LR - lev_dev - 1)))
    hmat = hmat.reshape(KP, nl * LR).T
    placed = jnp.stack(
        [jnp.pad(hmat, ((0, 0), (jj * KP, WIDE - (jj + 1) * KP))) for jj in range(JJ)]
    )

    coef = exchange(four, placed, nb, nl)
    per_device = src_blocks.shape[0]
    pool_block = src_blocks - (band - 1) * per_device
    return grid_part(
        pool_block, coef, waves(m_order, nb, slots), tap_index, tap_weight, nb, lev_dev
    )


def solution(mesh):
    in_specs = (
        P("band", None, None, "lev"),
        P("band", None, None),
        P("band", None, None),
        P(),
        P("lev", None),
        P("lev"),
        P("band", None),
        P("band", None, None),
        P("band", None, None),
    )
    out_specs = P("band", "lev", None)
    return jax.shard_map(shards, mesh=mesh, in_specs=in_specs, out_specs=out_specs, check_vma=False)
```

```python
import functools
import math

import jax
import jax.numpy as jnp
from jax import lax
from jax.experimental import pallas as pl
from jax.experimental.pallas import tpu as pltpu
from jax.sharding import PartitionSpec as P

NLON = 5120
BLK = 128
SLOTS = 4
TAPS = 4
XB = NLON // BLK
SP = 24
RS = 2 * SP
LR = 48
KP = 40
JJ = 6
WIDE = 256
MESH = pl.DeviceIdType.MESH


def exchange_kernel(nb, nl, f_ref, h_ref, out_ref, fall, ft, pieces, h, sa, ra, sb, rb):
    band = lax.axis_index("band")
    lev = lax.axis_index("lev")
    barrier = pltpu.get_barrier_semaphore()

    def greet_lev(i, _):
        pl.semaphore_signal(
            barrier, inc=1, device_id=(band, lax.rem(lev + i, nl)), device_id_type=MESH
        )
        return 0

    def greet_band(i, _):
        pl.semaphore_signal(
            barrier, inc=1, device_id=(lax.rem(band + i, nb), lev), device_id_type=MESH
        )
        return 0

    lax.fori_loop(1, nl, greet_lev, 0)
    lax.fori_loop(1, nb, greet_band, 0)
    pl.semaphore_wait(barrier, nl - 1 + nb - 1)

    def copy_a(i):
        peer = lax.rem(lev + i, nl)
        return pltpu.make_async_remote_copy(
            src_ref=f_ref,
            dst_ref=fall.at[lev],
            send_sem=sa.at[i],
            recv_sem=ra.at[i],
            device_id=(band, peer),
            device_id_type=MESH,
        )

    for i in range(1, nl):
        copy_a(i).start()
    width = f_ref.shape[1]
    edge = 2 * RS
    zero = jnp.zeros((edge, nl * LR), jnp.bfloat16)
    wide = h_ref[...].astype(jnp.float32)
    for jj in range(JJ):
        h[jj] = (wide if jj == 0 else pltpu.roll(wide, jj * KP, 1)).astype(jnp.bfloat16)
    ft[0:edge, :] = zero
    ft[edge + width : edge + width + edge, :] = zero
    fall[lev] = f_ref[...]
    for i in range(1, nl):
        copy_a(i).wait()
    step = 768
    for c in range(0, width, step):
        part = fall[:, :, c : c + step].reshape(nl * LR, step).astype(jnp.float32)
        ft[edge + c : edge + c + step, :] = part.T.astype(jnp.bfloat16)

    def make(b, _):
        total = jnp.zeros((RS, WIDE), jnp.float32)
        for jj in range(JJ):
            rows = ft[pl.ds(pl.multiple_of((2 * b + jj) * RS, 16), RS), :]
            total = total + jnp.dot(rows, h[jj], preferred_element_type=jnp.float32)
        pieces[b] = total.astype(jnp.bfloat16)
        return 0

    lax.fori_loop(0, nb, make, 0)

    def copy_b(i):
        peer = lax.rem(band + i, nb)
        return pltpu.make_async_remote_copy(
            src_ref=pieces.at[peer],
            dst_ref=out_ref.at[band],
            send_sem=sb.at[i],
            recv_sem=rb.at[i],
            device_id=(peer, lev),
            device_id_type=MESH,
        )

    def send(i, _):
        copy_b(i).start()
        return 0

    lax.fori_loop(1, nb, send, 0)
    out_ref[band] = pieces[band]

    def done(i, _):
        copy_b(i).wait()
        return 0

    lax.fori_loop(1, nb, done, 0)


def exchange(f, h, nb, nl):
    width = f.shape[1]
    vmem = pl.BlockSpec(memory_space=pltpu.VMEM)
    return pl.pallas_call(
        functools.partial(exchange_kernel, nb, nl),
        out_shape=jax.ShapeDtypeStruct((nb, RS, WIDE), jnp.bfloat16),
        in_specs=[vmem, vmem],
        out_specs=vmem,
        scratch_shapes=[
            pltpu.VMEM((nl, LR, width), jnp.bfloat16),
            pltpu.VMEM((width + 4 * RS, nl * LR), jnp.bfloat16),
            pltpu.VMEM((nb, RS, WIDE), jnp.bfloat16),
            pltpu.VMEM((JJ, nl * LR, WIDE), jnp.bfloat16),
            pltpu.SemaphoreType.DMA((nl,)),
            pltpu.SemaphoreType.DMA((nl,)),
            pltpu.SemaphoreType.DMA((nb,)),
            pltpu.SemaphoreType.DMA((nb,)),
        ],
        compiler_params=pltpu.CompilerParams(
            collective_id=0, has_side_effects=True, vmem_limit_bytes=41943040
        ),
    )(f, h)


def angle(phase):
    phase = phase - NLON * jnp.floor(phase * (1.0 / NLON))
    return phase * (2.0 * math.pi / NLON)


def grid_kernel(nb, lev_dev, src_ref, coef_ref, wave_ref, idx_ref, wgt_ref, out_ref, table, pool):
    def build(b, _):
        rows = pl.ds(pl.multiple_of(b * SP, 8), SP)
        orders = jnp.broadcast_to(wave_ref[rows, :], (SP, BLK))
        points = lax.broadcasted_iota(jnp.int32, (SP, BLK), 1).astype(jnp.float32)
        start, turn = angle(orders * points), angle(orders * float(BLK))
        factor = jnp.where(orders < 0.0, 0.0, jnp.where(orders == 0.0, 1.0, 2.0))
        real, imag = factor * jnp.cos(start), factor * jnp.sin(start)
        turn_c, turn_s = jnp.cos(turn), jnp.sin(turn)
        place = pl.ds(pl.multiple_of(b * RS, 16), RS)
        for x in range(XB):
            both = jnp.concatenate([real, -imag], axis=0)
            table[place, x * BLK : (x + 1) * BLK] = both.astype(jnp.bfloat16)
            real, imag = real * turn_c - imag * turn_s, imag * turn_c + real * turn_s
        return 0

    lax.fori_loop(0, nb, build, 0)
    coef = coef_ref[...].reshape(nb * RS, WIDE).astype(jnp.float32).T.astype(jnp.bfloat16)
    group = 4

    def synth(c, _):
        cols = pl.ds(pl.multiple_of(c * (group * BLK), 128), group * BLK)
        grid = jnp.dot(coef, table[:, cols], preferred_element_type=jnp.float32)
        for jj in range(JJ):
            for g in range(group):
                pool[jj * XB + c * group + g] = grid[
                    jj * KP : (jj + 1) * KP, g * BLK : (g + 1) * BLK
                ]
        return 0

    lax.fori_loop(0, XB // group, synth, 0)
    half = 2 * BLK
    cells = lax.broadcasted_iota(jnp.int32, (half, BLK), 0).astype(jnp.bfloat16)
    zero = jnp.zeros((half, BLK), jnp.bfloat16)

    def read(b):
        idx = idx_ref[b]
        wgt = wgt_ref[b].astype(jnp.bfloat16)
        total = None
        for h in range(2):
            spot = (idx - h * half).astype(jnp.float32).astype(jnp.bfloat16)
            spread = zero
            for t in range(TAPS):
                hit = cells == jnp.broadcast_to(spot[t : t + 1, :], (half, BLK))
                spread = spread + jnp.where(
                    hit, jnp.broadcast_to(wgt[t : t + 1, :], (half, BLK)), zero
                )
            source = jnp.concatenate(
                [pool[src_ref[b, 2 * h]], pool[src_ref[b, 2 * h + 1]]], axis=1
            ).astype(jnp.bfloat16)
            part = jnp.dot(source, spread, preferred_element_type=jnp.float32)
            total = part if total is None else total + part
        return total

    for j in range(2):

        def step(x, _):
            for u in range(4):
                xb = x * 4 + u
                out_ref[:, j, pl.ds(pl.multiple_of(xb * BLK, 128), BLK)] = read(j * XB + xb)[
                    :lev_dev
                ]
            return 0

        lax.fori_loop(0, XB // 4, step, 0)


def grid_part(src, coef, wave, idx, wgt, nb, lev_dev):
    vmem = pl.BlockSpec(memory_space=pltpu.VMEM)
    return pl.pallas_call(
        functools.partial(grid_kernel, nb, lev_dev),
        out_shape=jax.ShapeDtypeStruct((lev_dev, 2, NLON), jnp.float32),
        in_specs=[pl.BlockSpec(memory_space=pltpu.SMEM)] + [vmem] * 4,
        out_specs=vmem,
        scratch_shapes=[
            pltpu.VMEM((nb * RS, NLON), jnp.bfloat16),
            pltpu.VMEM((JJ * XB, KP, BLK), jnp.float32),
        ],
        compiler_params=pltpu.CompilerParams(vmem_limit_bytes=58720256),
    )(src, coef, wave, idx, wgt)


def waves(m_order, nb, slots):
    orders = m_order.astype(jnp.float32).reshape(nb, slots)
    orders = jnp.pad(orders, ((0, 0), (0, SP - slots)), constant_values=-1.0)
    return orders.reshape(nb * SP, 1)


def shards(
    temp_spectrum,
    surf_spectrum,
    legendre,
    m_order,
    hydro_matrix,
    surf_coupling,
    src_blocks,
    tap_index,
    tap_weight,
):
    slots, n_count, _, lev_dev = temp_spectrum.shape
    lat_all = legendre.shape[1]
    nb, nl = lax.axis_size("band"), lax.axis_size("lev")
    band, lev = lax.axis_index("band"), lax.axis_index("lev")
    my_orders = lax.dynamic_slice_in_dim(m_order, band * slots, slots)
    n_index = jnp.arange(n_count, dtype=jnp.int32)
    keep = n_index[None, None, :] >= my_orders[:, None, None]
    values = jnp.where(keep, legendre, jnp.zeros_like(legendre))
    four_t = jnp.einsum(
        "sjn,snrk->sjrk", values, temp_spectrum, preferred_element_type=jnp.float32
    ).astype(jnp.bfloat16)
    four_p = jnp.einsum(
        "sjn,snr->sjr", values, surf_spectrum, preferred_element_type=jnp.float32
    ).astype(jnp.bfloat16)
    four = jnp.concatenate([four_t, four_p[..., None]], axis=3)
    four = jnp.transpose(four, (3, 1, 2, 0))
    four = jnp.pad(four, ((0, LR - lev_dev - 1), (0, 0), (0, 0), (0, SP - slots)))
    four = four.reshape(LR, lat_all * RS)

    lev_total = hydro_matrix.shape[1]
    rows = lax.broadcasted_iota(jnp.int32, (lev_dev, lev_total), 0) + lev * lev_dev
    cols = lax.broadcasted_iota(jnp.int32, (lev_dev, lev_total), 1)
    hmat = jnp.where(cols >= rows, hydro_matrix, jnp.zeros_like(hydro_matrix))
    hmat = hmat.reshape(lev_dev, nl, lev_dev)
    surf = jnp.where(jnp.arange(nl)[None, :] == lev, surf_coupling[:, None], 0.0)
    hmat = jnp.concatenate([hmat, surf.astype(jnp.bfloat16)[:, :, None]], axis=2)
    hmat = jnp.pad(hmat, ((0, KP - lev_dev), (0, 0), (0, LR - lev_dev - 1)))
    hmat = hmat.reshape(KP, nl * LR).T
    placed = jnp.pad(hmat, ((0, 0), (0, WIDE - KP)))

    coef = exchange(four, placed, nb, nl)
    per_device = src_blocks.shape[0]
    pool_block = src_blocks - (band - 1) * per_device
    out = grid_part(
        pool_block, coef, waves(m_order, nb, slots), tap_index, tap_weight, nb, lev_dev
    )
    return jnp.transpose(out, (1, 0, 2))


def solution(mesh):
    in_specs = (
        P("band", None, None, "lev"),
        P("band", None, None),
        P("band", None, None),
        P(),
        P("lev", None),
        P("lev"),
        P("band", None),
        P("band", None, None),
        P("band", None, None),
    )
    out_specs = P("band", "lev", None)
    return jax.shard_map(shards, mesh=mesh, in_specs=in_specs, out_specs=out_specs, check_vma=False)
```

```python
import functools
import math

import jax
import jax.numpy as jnp
from jax import lax
from jax.experimental import pallas as pl
from jax.experimental.pallas import tpu as pltpu
from jax.sharding import PartitionSpec as P

NLON = 5120
BLK = 128
SLOTS = 4
TAPS = 4
XB = NLON // BLK
SP = 24
RS = 2 * SP
LR = 48
KP = 40
JJ = 6
WIDE = 256
MESH = pl.DeviceIdType.MESH


def exchange_kernel(nb, nl, f_ref, h_ref, out_ref, fall, ft, pieces, h, sa, ra, sb, rb):
    band = lax.axis_index("band")
    lev = lax.axis_index("lev")
    barrier = pltpu.get_barrier_semaphore()

    def greet_lev(i, _):
        pl.semaphore_signal(
            barrier, inc=1, device_id=(band, lax.rem(lev + i, nl)), device_id_type=MESH
        )
        return 0

    def greet_band(i, _):
        pl.semaphore_signal(
            barrier, inc=1, device_id=(lax.rem(band + i, nb), lev), device_id_type=MESH
        )
        return 0

    lax.fori_loop(1, nl, greet_lev, 0)
    lax.fori_loop(1, nb, greet_band, 0)
    pl.semaphore_wait(barrier, nl - 1 + nb - 1)

    def copy_a(i):
        peer = lax.rem(lev + i, nl)
        return pltpu.make_async_remote_copy(
            src_ref=f_ref,
            dst_ref=fall.at[lev],
            send_sem=sa.at[i],
            recv_sem=ra.at[i],
            device_id=(band, peer),
            device_id_type=MESH,
        )

    for i in range(1, nl):
        copy_a(i).start()
    width = f_ref.shape[1]
    edge = 2 * RS
    zero = jnp.zeros((edge + RS, nl * LR), jnp.bfloat16)
    wide = h_ref[...].astype(jnp.float32)
    for jj in range(JJ):
        h[jj] = (wide if jj == 0 else pltpu.roll(wide, jj * KP, 1)).astype(jnp.bfloat16)
    ft[0:edge, :] = zero[:edge]
    ft[edge + width : edge + width + edge + RS, :] = zero
    fall[lev] = f_ref[...]
    for i in range(1, nl):
        copy_a(i).wait()
    step = 768
    for c in range(0, width, step):
        part = fall[:, :, c : c + step].reshape(nl * LR, step).astype(jnp.float32)
        ft[edge + c : edge + c + step, :] = part.T.astype(jnp.bfloat16)

    batch = math.gcd(nb, 8)
    span = batch * 2 * RS

    def make(g, _):
        total = jnp.zeros((batch * RS, WIDE), jnp.float32)
        for jj in range(JJ):
            rows = ft[pl.ds(pl.multiple_of(g * span + jj * RS, 16), span), :]
            rows = rows.reshape(batch, 2 * RS, nl * LR)[:, :RS].reshape(batch * RS, nl * LR)
            total = total + jnp.dot(rows, h[jj], preferred_element_type=jnp.float32)
        pieces[pl.ds(g * batch, batch)] = total.astype(jnp.bfloat16).reshape(batch, RS, WIDE)
        return 0

    lax.fori_loop(0, nb // batch, make, 0)

    def copy_b(i):
        peer = lax.rem(band + i, nb)
        return pltpu.make_async_remote_copy(
            src_ref=pieces.at[peer],
            dst_ref=out_ref.at[band],
            send_sem=sb.at[i],
            recv_sem=rb.at[i],
            device_id=(peer, lev),
            device_id_type=MESH,
        )

    def send(i, _):
        copy_b(i).start()
        return 0

    lax.fori_loop(1, nb, send, 0)
    out_ref[band] = pieces[band]

    def done(i, _):
        copy_b(i).wait()
        return 0

    lax.fori_loop(1, nb, done, 0)


def exchange(f, h, nb, nl):
    width = f.shape[1]
    vmem = pl.BlockSpec(memory_space=pltpu.VMEM)
    return pl.pallas_call(
        functools.partial(exchange_kernel, nb, nl),
        out_shape=jax.ShapeDtypeStruct((nb, RS, WIDE), jnp.bfloat16),
        in_specs=[vmem, vmem],
        out_specs=vmem,
        scratch_shapes=[
            pltpu.VMEM((nl, LR, width), jnp.bfloat16),
            pltpu.VMEM((width + 5 * RS, nl * LR), jnp.bfloat16),
            pltpu.VMEM((nb, RS, WIDE), jnp.bfloat16),
            pltpu.VMEM((JJ, nl * LR, WIDE), jnp.bfloat16),
            pltpu.SemaphoreType.DMA((nl,)),
            pltpu.SemaphoreType.DMA((nl,)),
            pltpu.SemaphoreType.DMA((nb,)),
            pltpu.SemaphoreType.DMA((nb,)),
        ],
        compiler_params=pltpu.CompilerParams(
            collective_id=0, has_side_effects=True, vmem_limit_bytes=41943040
        ),
    )(f, h)


def angle(phase):
    phase = phase - NLON * jnp.floor(phase * (1.0 / NLON))
    return phase * (2.0 * math.pi / NLON)


def grid_kernel(nb, lev_dev, src_ref, coef_ref, wave_ref, idx_ref, wgt_ref, out_ref, table, pool):
    def build(b, _):
        rows = pl.ds(pl.multiple_of(b * SP, 8), SP)
        orders = jnp.broadcast_to(wave_ref[rows, :], (SP, BLK))
        points = lax.broadcasted_iota(jnp.int32, (SP, BLK), 1).astype(jnp.float32)
        start, turn = angle(orders * points), angle(orders * float(BLK))
        factor = jnp.where(orders < 0.0, 0.0, jnp.where(orders == 0.0, 1.0, 2.0))
        real, imag = factor * jnp.cos(start), factor * jnp.sin(start)
        turn_c, turn_s = jnp.cos(turn), jnp.sin(turn)
        place = pl.ds(pl.multiple_of(b * RS, 16), RS)
        for x in range(XB):
            both = jnp.concatenate([real, -imag], axis=0)
            table[place, x * BLK : (x + 1) * BLK] = both.astype(jnp.bfloat16)
            real, imag = real * turn_c - imag * turn_s, imag * turn_c + real * turn_s
        return 0

    lax.fori_loop(0, nb, build, 0)
    coef = coef_ref[...].reshape(nb * RS, WIDE).astype(jnp.float32).T.astype(jnp.bfloat16)
    group = 4

    def synth(c, _):
        cols = pl.ds(pl.multiple_of(c * (group * BLK), 128), group * BLK)
        grid = jnp.dot(coef, table[:, cols], preferred_element_type=jnp.float32)
        for jj in range(JJ):
            for g in range(group):
                pool[jj * XB + c * group + g] = grid[
                    jj * KP : (jj + 1) * KP, g * BLK : (g + 1) * BLK
                ]
        return 0

    lax.fori_loop(0, XB // group, synth, 0)
    half = 2 * BLK
    cells = lax.broadcasted_iota(jnp.int32, (half, BLK), 0).astype(jnp.bfloat16)
    zero = jnp.zeros((half, BLK), jnp.bfloat16)

    first = (lax.axis_index("band") - 1) * (2 * XB)

    def read(b):
        idx = idx_ref[b]
        wgt = wgt_ref[b].astype(jnp.bfloat16)
        total = None
        for h in range(2):
            spot = (idx - h * half).astype(jnp.float32).astype(jnp.bfloat16)
            spread = zero
            for t in range(TAPS):
                hit = cells == jnp.broadcast_to(spot[t : t + 1, :], (half, BLK))
                spread = spread + jnp.where(
                    hit, jnp.broadcast_to(wgt[t : t + 1, :], (half, BLK)), zero
                )
            source = jnp.concatenate(
                [pool[src_ref[2 * h, b] - first], pool[src_ref[2 * h + 1, b] - first]], axis=1
            ).astype(jnp.bfloat16)
            part = jnp.dot(source, spread, preferred_element_type=jnp.float32)
            total = part if total is None else total + part
        return total

    for j in range(2):

        def step(x, _):
            for u in range(4):
                xb = x * 4 + u
                out_ref[:, j, pl.ds(pl.multiple_of(xb * BLK, 128), BLK)] = read(j * XB + xb)[
                    :lev_dev
                ]
            return 0

        lax.fori_loop(0, XB // 4, step, 0)


def grid_part(src, coef, wave, idx, wgt, nb, lev_dev):
    vmem = pl.BlockSpec(memory_space=pltpu.VMEM)
    return pl.pallas_call(
        functools.partial(grid_kernel, nb, lev_dev),
        out_shape=jax.ShapeDtypeStruct((lev_dev, 2, NLON), jnp.float32),
        in_specs=[pl.BlockSpec(memory_space=pltpu.SMEM)] + [vmem] * 4,
        out_specs=vmem,
        scratch_shapes=[
            pltpu.VMEM((nb * RS, NLON), jnp.bfloat16),
            pltpu.VMEM((JJ * XB, KP, BLK), jnp.float32),
        ],
        compiler_params=pltpu.CompilerParams(vmem_limit_bytes=58720256),
    )(src, coef, wave, idx, wgt)


def waves(m_order, nb, slots):
    orders = m_order.astype(jnp.float32).reshape(nb, slots)
    orders = jnp.pad(orders, ((0, 0), (0, SP - slots)), constant_values=-1.0)
    return orders.reshape(nb * SP, 1)


def shards(
    temp_spectrum,
    surf_spectrum,
    legendre,
    m_order,
    hydro_matrix,
    surf_coupling,
    src_blocks,
    tap_index,
    tap_weight,
):
    slots, n_count, _, lev_dev = temp_spectrum.shape
    lat_all = legendre.shape[1]
    nb, nl = lax.axis_size("band"), lax.axis_size("lev")
    band, lev = lax.axis_index("band"), lax.axis_index("lev")
    my_orders = lax.dynamic_slice_in_dim(m_order, band * slots, slots)
    n_index = jnp.arange(n_count, dtype=jnp.int32)
    keep = n_index[None, None, :] >= my_orders[:, None, None]
    values = jnp.where(keep, legendre, jnp.zeros_like(legendre))
    four_t = jnp.einsum(
        "sjn,snrk->sjrk", values, temp_spectrum, preferred_element_type=jnp.float32
    ).astype(jnp.bfloat16)
    four_p = jnp.einsum(
        "sjn,snr->sjr", values, surf_spectrum, preferred_element_type=jnp.float32
    ).astype(jnp.bfloat16)
    four = jnp.concatenate([four_t, four_p[..., None]], axis=3)
    four = jnp.transpose(four, (3, 1, 2, 0))
    four = jnp.pad(four, ((0, LR - lev_dev - 1), (0, 0), (0, 0), (0, SP - slots)))
    four = four.reshape(LR, lat_all * RS)

    lev_total = hydro_matrix.shape[1]
    rows = lax.broadcasted_iota(jnp.int32, (lev_dev, lev_total), 0) + lev * lev_dev
    cols = lax.broadcasted_iota(jnp.int32, (lev_dev, lev_total), 1)
    hmat = jnp.where(cols >= rows, hydro_matrix, jnp.zeros_like(hydro_matrix))
    hmat = hmat.reshape(lev_dev, nl, lev_dev)
    surf = jnp.where(jnp.arange(nl)[None, :] == lev, surf_coupling[:, None], 0.0)
    hmat = jnp.concatenate([hmat, surf.astype(jnp.bfloat16)[:, :, None]], axis=2)
    hmat = jnp.pad(hmat, ((0, KP - lev_dev), (0, 0), (0, LR - lev_dev - 1)))
    hmat = hmat.reshape(KP, nl * LR).T
    placed = jnp.pad(hmat, ((0, 0), (0, WIDE - KP)))

    coef = exchange(four, placed, nb, nl)
    out = grid_part(
        src_blocks.T, coef, waves(m_order, nb, slots), tap_index, tap_weight, nb, lev_dev
    )
    return jnp.transpose(out, (1, 0, 2))


def solution(mesh):
    in_specs = (
        P("band", None, None, "lev"),
        P("band", None, None),
        P("band", None, None),
        P(),
        P("lev", None),
        P("lev"),
        P("band", None),
        P("band", None, None),
        P("band", None, None),
    )
    out_specs = P("band", "lev", None)
    return jax.shard_map(shards, mesh=mesh, in_specs=in_specs, out_specs=out_specs, check_vma=False)
```

```python
import functools
import math

import jax
import jax.numpy as jnp
from jax import lax
from jax.experimental import pallas as pl
from jax.experimental.pallas import tpu as pltpu
from jax.sharding import PartitionSpec as P

NLON = 5120
BLK = 128
SLOTS = 4
TAPS = 4
XB = NLON // BLK
SP = 24
RS = 2 * SP
LR = 48
KP = 40
JJ = 6
WIDE = 256
MESH = pl.DeviceIdType.MESH


def exchange_kernel(nb, nl, f_ref, h_ref, s_ref, out_ref, fall, ft, pieces, h, sa, ra, sb, rb):
    band = lax.axis_index("band")
    lev = lax.axis_index("lev")
    barrier = pltpu.get_barrier_semaphore()

    def greet_lev(i, _):
        pl.semaphore_signal(
            barrier, inc=1, device_id=(band, lax.rem(lev + i, nl)), device_id_type=MESH
        )
        return 0

    def greet_band(i, _):
        pl.semaphore_signal(
            barrier, inc=1, device_id=(lax.rem(band + i, nb), lev), device_id_type=MESH
        )
        return 0

    lax.fori_loop(1, nl, greet_lev, 0)
    lax.fori_loop(1, nb, greet_band, 0)
    pl.semaphore_wait(barrier, nl - 1 + nb - 1)

    def copy_a(i):
        peer = lax.rem(lev + i, nl)
        return pltpu.make_async_remote_copy(
            src_ref=f_ref,
            dst_ref=fall.at[lev],
            send_sem=sa.at[i],
            recv_sem=ra.at[i],
            device_id=(band, peer),
            device_id_type=MESH,
        )

    for i in range(1, nl):
        copy_a(i).start()
    width = f_ref.shape[1]
    edge = 2 * RS
    zero = jnp.zeros((edge + RS, nl * LR), jnp.bfloat16)
    lev_dev, lev_total = h_ref.shape
    row = lax.broadcasted_iota(jnp.int32, (lev_dev, lev_total), 0) + lev * lev_dev
    col = lax.broadcasted_iota(jnp.int32, (lev_dev, lev_total), 1)
    upper = jnp.where(col >= row, h_ref[...].astype(jnp.float32), 0.0).astype(jnp.bfloat16)
    row = lax.broadcasted_iota(jnp.int32, (nl * LR, lev_total), 0)
    col = lax.broadcasted_iota(jnp.int32, (nl * LR, lev_total), 1)
    spots = jnp.zeros((nl * LR, lev_total), jnp.float32)
    for v in range(nl):
        inside = (row >= v * LR) & (row < v * LR + lev_dev)
        spots = jnp.where(inside & (col == row - v * (LR - lev_dev)), 1.0, spots)
    tall = lax.dot_general(
        spots.astype(jnp.bfloat16),
        upper,
        (((1,), (1,)), ((), ())),
        preferred_element_type=jnp.float32,
    )
    row = lax.broadcasted_iota(jnp.int32, (nl * LR, lev_dev), 0)
    surf = jnp.broadcast_to(s_ref[...], (nl * LR, lev_dev))
    tall = jnp.where(row == lev * LR + lev_dev, surf, tall).astype(jnp.bfloat16)
    row = lax.broadcasted_iota(jnp.int32, (lev_dev, WIDE), 0)
    col = lax.broadcasted_iota(jnp.int32, (lev_dev, WIDE), 1)
    for jj in range(JJ):
        place = jnp.where(col == row + jj * KP, 1.0, 0.0).astype(jnp.bfloat16)
        h[jj] = jnp.dot(tall, place, preferred_element_type=jnp.float32).astype(jnp.bfloat16)
    ft[0:edge, :] = zero[:edge]
    ft[edge + width : edge + width + edge + RS, :] = zero
    fall[lev] = f_ref[...]
    for i in range(1, nl):
        copy_a(i).wait()
    step = 768
    for c in range(0, width, step):
        part = fall[:, :, c : c + step].reshape(nl * LR, step).astype(jnp.float32)
        ft[edge + c : edge + c + step, :] = part.T.astype(jnp.bfloat16)

    batch = math.gcd(nb, 8)
    span = batch * 2 * RS

    def make(g, _):
        total = jnp.zeros((batch * RS, WIDE), jnp.float32)
        for jj in range(JJ):
            rows = ft[pl.ds(pl.multiple_of(g * span + jj * RS, 16), span), :]
            rows = rows.reshape(batch, 2 * RS, nl * LR)[:, :RS].reshape(batch * RS, nl * LR)
            total = total + jnp.dot(rows, h[jj], preferred_element_type=jnp.float32)
        pieces[pl.ds(g * batch, batch)] = total.astype(jnp.bfloat16).reshape(batch, RS, WIDE)
        return 0

    lax.fori_loop(0, nb // batch, make, 0)

    def copy_b(i):
        peer = lax.rem(band + i, nb)
        return pltpu.make_async_remote_copy(
            src_ref=pieces.at[peer],
            dst_ref=out_ref.at[band],
            send_sem=sb.at[i],
            recv_sem=rb.at[i],
            device_id=(peer, lev),
            device_id_type=MESH,
        )

    def send(i, _):
        copy_b(i).start()
        return 0

    lax.fori_loop(1, nb, send, 0)
    out_ref[band] = pieces[band]

    def done(i, _):
        copy_b(i).wait()
        return 0

    lax.fori_loop(1, nb, done, 0)


def exchange(f, h, s, nb, nl):
    width = f.shape[1]
    vmem = pl.BlockSpec(memory_space=pltpu.VMEM)
    return pl.pallas_call(
        functools.partial(exchange_kernel, nb, nl),
        out_shape=jax.ShapeDtypeStruct((nb, RS, WIDE), jnp.bfloat16),
        in_specs=[vmem, vmem, vmem],
        out_specs=vmem,
        scratch_shapes=[
            pltpu.VMEM((nl, LR, width), jnp.bfloat16),
            pltpu.VMEM((width + 5 * RS, nl * LR), jnp.bfloat16),
            pltpu.VMEM((nb, RS, WIDE), jnp.bfloat16),
            pltpu.VMEM((JJ, nl * LR, WIDE), jnp.bfloat16),
            pltpu.SemaphoreType.DMA((nl,)),
            pltpu.SemaphoreType.DMA((nl,)),
            pltpu.SemaphoreType.DMA((nb,)),
            pltpu.SemaphoreType.DMA((nb,)),
        ],
        compiler_params=pltpu.CompilerParams(
            collective_id=0, has_side_effects=True, vmem_limit_bytes=41943040
        ),
    )(f, h, s)


def angle(phase):
    phase = phase - NLON * jnp.floor(phase * (1.0 / NLON))
    return phase * (2.0 * math.pi / NLON)


def grid_kernel(nb, lev_dev, src_ref, coef_ref, wave_ref, idx_ref, wgt_ref, out_ref, table, pool):
    pair = math.gcd(nb, 2)
    tall = pair * SP

    def build(b, _):
        rows = pl.ds(pl.multiple_of(b * tall, 8), tall)
        orders = jnp.broadcast_to(wave_ref[rows, :], (tall, BLK))
        points = lax.broadcasted_iota(jnp.int32, (tall, BLK), 1).astype(jnp.float32)
        start, turn = angle(orders * points), angle(orders * float(BLK))
        factor = jnp.where(orders < 0.0, 0.0, jnp.where(orders == 0.0, 1.0, 2.0))
        real, imag = factor * jnp.cos(start), factor * jnp.sin(start)
        turn_c, turn_s = jnp.cos(turn), jnp.sin(turn)
        place = pl.ds(pl.multiple_of(b * pair * RS, 16), pair * RS)
        for x in range(XB):
            parts = []
            for u in range(pair):
                own = slice(u * SP, (u + 1) * SP)
                parts += [real[own], -imag[own]]
            both = jnp.concatenate(parts, axis=0)
            table[place, x * BLK : (x + 1) * BLK] = both.astype(jnp.bfloat16)
            real, imag = real * turn_c - imag * turn_s, imag * turn_c + real * turn_s
        return 0

    lax.fori_loop(0, nb // pair, build, 0)
    coef = coef_ref[...].reshape(nb * RS, WIDE).astype(jnp.float32).T.astype(jnp.bfloat16)
    group = 4

    def synth(c, _):
        cols = pl.ds(pl.multiple_of(c * (group * BLK), 128), group * BLK)
        grid = jnp.dot(coef, table[:, cols], preferred_element_type=jnp.float32)
        for jj in range(JJ):
            for g in range(group):
                pool[jj * XB + c * group + g] = grid[
                    jj * KP : (jj + 1) * KP, g * BLK : (g + 1) * BLK
                ]
        return 0

    lax.fori_loop(0, XB // group, synth, 0)
    half = 2 * BLK
    cells = lax.broadcasted_iota(jnp.int32, (half, BLK), 0).astype(jnp.bfloat16)
    zero = jnp.zeros((half, BLK), jnp.bfloat16)

    first = (lax.axis_index("band") - 1) * (2 * XB)

    def read(b):
        idx = idx_ref[b]
        wgt = wgt_ref[b].astype(jnp.bfloat16)
        total = None
        for h in range(2):
            spot = (idx - h * half).astype(jnp.float32).astype(jnp.bfloat16)
            spread = zero
            for t in range(TAPS):
                hit = cells == jnp.broadcast_to(spot[t : t + 1, :], (half, BLK))
                spread = spread + jnp.where(
                    hit, jnp.broadcast_to(wgt[t : t + 1, :], (half, BLK)), zero
                )
            source = jnp.concatenate(
                [pool[src_ref[2 * h, b] - first], pool[src_ref[2 * h + 1, b] - first]], axis=1
            ).astype(jnp.bfloat16)
            part = jnp.dot(source, spread, preferred_element_type=jnp.float32)
            total = part if total is None else total + part
        return total

    for j in range(2):

        def step(x, _):
            for u in range(4):
                xb = x * 4 + u
                out_ref[:, j, pl.ds(pl.multiple_of(xb * BLK, 128), BLK)] = read(j * XB + xb)[
                    :lev_dev
                ]
            return 0

        lax.fori_loop(0, XB // 4, step, 0)


def grid_part(src, coef, wave, idx, wgt, nb, lev_dev):
    vmem = pl.BlockSpec(memory_space=pltpu.VMEM)
    return pl.pallas_call(
        functools.partial(grid_kernel, nb, lev_dev),
        out_shape=jax.ShapeDtypeStruct((lev_dev, 2, NLON), jnp.float32),
        in_specs=[pl.BlockSpec(memory_space=pltpu.SMEM)] + [vmem] * 4,
        out_specs=vmem,
        scratch_shapes=[
            pltpu.VMEM((nb * RS, NLON), jnp.bfloat16),
            pltpu.VMEM((JJ * XB, KP, BLK), jnp.float32),
        ],
        compiler_params=pltpu.CompilerParams(vmem_limit_bytes=58720256),
    )(src, coef, wave, idx, wgt)


def waves(m_order, nb, slots):
    orders = m_order.astype(jnp.float32).reshape(nb, slots)
    orders = jnp.pad(orders, ((0, 0), (0, SP - slots)), constant_values=-1.0)
    return orders.reshape(nb * SP, 1)


def shards(
    temp_spectrum,
    surf_spectrum,
    legendre,
    m_order,
    hydro_matrix,
    surf_coupling,
    src_blocks,
    tap_index,
    tap_weight,
):
    slots, n_count, _, lev_dev = temp_spectrum.shape
    lat_all = legendre.shape[1]
    nb, nl = lax.axis_size("band"), lax.axis_size("lev")
    band = lax.axis_index("band")
    my_orders = lax.dynamic_slice_in_dim(m_order, band * slots, slots)
    n_index = jnp.arange(n_count, dtype=jnp.int32)
    keep = n_index[None, None, :] >= my_orders[:, None, None]
    values = jnp.where(keep, legendre, jnp.zeros_like(legendre))
    four_t = jnp.einsum(
        "sjn,snrk->sjrk", values, temp_spectrum, preferred_element_type=jnp.float32
    ).astype(jnp.bfloat16)
    four_p = jnp.einsum(
        "sjn,snr->sjr", values, surf_spectrum, preferred_element_type=jnp.float32
    ).astype(jnp.bfloat16)
    four = jnp.concatenate([four_t, four_p[..., None]], axis=3)
    four = jnp.transpose(four, (3, 1, 2, 0))
    four = jnp.pad(four, ((0, LR - lev_dev - 1), (0, 0), (0, 0), (0, SP - slots)))
    four = four.reshape(LR, lat_all * RS)

    coef = exchange(four, hydro_matrix, surf_coupling[None, :], nb, nl)
    out = grid_part(
        src_blocks.T, coef, waves(m_order, nb, slots), tap_index, tap_weight, nb, lev_dev
    )
    return jnp.transpose(out, (1, 0, 2))


def solution(mesh):
    in_specs = (
        P("band", None, None, "lev"),
        P("band", None, None),
        P("band", None, None),
        P(),
        P("lev", None),
        P("lev"),
        P("band", None),
        P("band", None, None),
        P("band", None, None),
    )
    out_specs = P("band", "lev", None)
    return jax.shard_map(shards, mesh=mesh, in_specs=in_specs, out_specs=out_specs, check_vma=False)
```

```python
import functools
import math

import jax
import jax.numpy as jnp
from jax import lax
from jax.experimental import pallas as pl
from jax.experimental.pallas import tpu as pltpu
from jax.sharding import PartitionSpec as P

NLON = 5120
BLK = 128
SLOTS = 4
TAPS = 4
XB = NLON // BLK
SP = 24
RS = 2 * SP
LR = 48
KP = 40
JJ = 6
WIDE = 256
MESH = pl.DeviceIdType.MESH


def exchange_kernel(nb, nl, f_ref, h_ref, s_ref, out_ref, fall, ft, pieces, h, sa, ra, sb, rb):
    band = lax.axis_index("band")
    lev = lax.axis_index("lev")
    barrier = pltpu.get_barrier_semaphore()

    def greet_lev(i, _):
        pl.semaphore_signal(
            barrier, inc=1, device_id=(band, lax.rem(lev + i, nl)), device_id_type=MESH
        )
        return 0

    def greet_band(i, _):
        pl.semaphore_signal(
            barrier, inc=1, device_id=(lax.rem(band + i, nb), lev), device_id_type=MESH
        )
        return 0

    lax.fori_loop(1, nl, greet_lev, 0)
    lax.fori_loop(1, nb, greet_band, 0)
    pl.semaphore_wait(barrier, nl - 1 + nb - 1)

    def copy_a(i):
        peer = lax.rem(lev + i, nl)
        return pltpu.make_async_remote_copy(
            src_ref=f_ref,
            dst_ref=fall.at[lev],
            send_sem=sa.at[i],
            recv_sem=ra.at[i],
            device_id=(band, peer),
            device_id_type=MESH,
        )

    for i in range(1, nl):
        copy_a(i).start()
    width = f_ref.shape[1]
    edge = 2 * RS
    zero = jnp.zeros((edge + RS, nl * LR), jnp.bfloat16)
    lev_dev, lev_total = h_ref.shape
    row = lax.broadcasted_iota(jnp.int32, (lev_dev, lev_total), 0) + lev * lev_dev
    col = lax.broadcasted_iota(jnp.int32, (lev_dev, lev_total), 1)
    upper = jnp.where(col >= row, h_ref[...].astype(jnp.float32), 0.0).astype(jnp.bfloat16)
    row = lax.broadcasted_iota(jnp.int32, (nl * LR, lev_total), 0)
    col = lax.broadcasted_iota(jnp.int32, (nl * LR, lev_total), 1)
    spots = jnp.zeros((nl * LR, lev_total), jnp.float32)
    for v in range(nl):
        inside = (row >= v * LR) & (row < v * LR + lev_dev)
        spots = jnp.where(inside & (col == row - v * (LR - lev_dev)), 1.0, spots)
    tall = lax.dot_general(
        spots.astype(jnp.bfloat16),
        upper,
        (((1,), (1,)), ((), ())),
        preferred_element_type=jnp.float32,
    )
    row = lax.broadcasted_iota(jnp.int32, (nl * LR, lev_dev), 0)
    surf = jnp.broadcast_to(s_ref[...], (nl * LR, lev_dev))
    tall = jnp.where(row == lev * LR + lev_dev, surf, tall).astype(jnp.bfloat16)
    row = lax.broadcasted_iota(jnp.int32, (lev_dev, WIDE), 0)
    col = lax.broadcasted_iota(jnp.int32, (lev_dev, WIDE), 1)
    for jj in range(JJ):
        place = jnp.where(col == row + jj * KP, 1.0, 0.0).astype(jnp.bfloat16)
        h[jj] = jnp.dot(tall, place, preferred_element_type=jnp.float32).astype(jnp.bfloat16)
    ft[0:edge, :] = zero[:edge]
    ft[edge + width : edge + width + edge + RS, :] = zero
    fall[lev] = f_ref[...]
    for i in range(1, nl):
        copy_a(i).wait()
    step = 768
    for c in range(0, width, step):
        part = fall[:, :, c : c + step].reshape(nl * LR, step).astype(jnp.float32)
        ft[edge + c : edge + c + step, :] = part.T.astype(jnp.bfloat16)

    batch = math.gcd(nb, 8)
    span = batch * 2 * RS

    def make(g, _):
        total = jnp.zeros((batch * RS, WIDE), jnp.float32)
        for jj in range(JJ):
            rows = ft[pl.ds(pl.multiple_of(g * span + jj * RS, 16), span), :]
            rows = rows.reshape(batch, 2 * RS, nl * LR)[:, :RS].reshape(batch * RS, nl * LR)
            total = total + jnp.dot(rows, h[jj], preferred_element_type=jnp.float32)
        pieces[pl.ds(g * batch, batch)] = total.astype(jnp.bfloat16).reshape(batch, RS, WIDE)
        return 0

    lax.fori_loop(0, nb // batch, make, 0)

    def copy_b(i):
        peer = lax.rem(band + i, nb)
        return pltpu.make_async_remote_copy(
            src_ref=pieces.at[peer],
            dst_ref=out_ref.at[band],
            send_sem=sb.at[i],
            recv_sem=rb.at[i],
            device_id=(peer, lev),
            device_id_type=MESH,
        )

    def send(i, _):
        copy_b(i).start()
        return 0

    lax.fori_loop(1, nb, send, 0)
    out_ref[band] = pieces[band]

    def done(i, _):
        copy_b(i).wait()
        return 0

    lax.fori_loop(1, nb, done, 0)


def exchange(f, h, s, nb, nl):
    width = f.shape[1]
    vmem = pl.BlockSpec(memory_space=pltpu.VMEM)
    return pl.pallas_call(
        functools.partial(exchange_kernel, nb, nl),
        out_shape=jax.ShapeDtypeStruct((nb, RS, WIDE), jnp.bfloat16),
        in_specs=[vmem, vmem, vmem],
        out_specs=vmem,
        scratch_shapes=[
            pltpu.VMEM((nl, LR, width), jnp.bfloat16),
            pltpu.VMEM((width + 5 * RS, nl * LR), jnp.bfloat16),
            pltpu.VMEM((nb, RS, WIDE), jnp.bfloat16),
            pltpu.VMEM((JJ, nl * LR, WIDE), jnp.bfloat16),
            pltpu.SemaphoreType.DMA((nl,)),
            pltpu.SemaphoreType.DMA((nl,)),
            pltpu.SemaphoreType.DMA((nb,)),
            pltpu.SemaphoreType.DMA((nb,)),
        ],
        compiler_params=pltpu.CompilerParams(
            collective_id=0, has_side_effects=True, vmem_limit_bytes=41943040
        ),
    )(f, h, s)


def angle(phase):
    phase = phase - NLON * jnp.floor(phase * (1.0 / NLON))
    return phase * (2.0 * math.pi / NLON)


def grid_kernel(nb, lev_dev, src_ref, coef_ref, wave_ref, idx_ref, wgt_ref, out_ref, table, pool):
    pair = math.gcd(nb, 2)
    tall = pair * SP

    def build(b, _):
        rows = pl.ds(pl.multiple_of(b * tall, 8), tall)
        orders = jnp.broadcast_to(wave_ref[rows, :], (tall, BLK))
        points = lax.broadcasted_iota(jnp.int32, (tall, BLK), 1).astype(jnp.float32)
        start, turn = angle(orders * points), angle(orders * float(BLK))
        factor = jnp.where(orders < 0.0, 0.0, jnp.where(orders == 0.0, 1.0, 2.0))
        real, imag = factor * jnp.cos(start), factor * jnp.sin(start)
        turn_c, turn_s = jnp.cos(turn), jnp.sin(turn)
        place = pl.ds(pl.multiple_of(b * pair * RS, 16), pair * RS)
        for x in range(XB):
            parts = []
            for u in range(pair):
                own = slice(u * SP, (u + 1) * SP)
                parts += [real[own], -imag[own]]
            both = jnp.concatenate(parts, axis=0)
            table[place, x * BLK : (x + 1) * BLK] = both.astype(jnp.bfloat16)
            real, imag = real * turn_c - imag * turn_s, imag * turn_c + real * turn_s
        return 0

    lax.fori_loop(0, nb // pair, build, 0)
    coef = coef_ref[...].reshape(nb * RS, WIDE).astype(jnp.float32).T.astype(jnp.bfloat16)
    group = 4

    def synth(c, _):
        cols = pl.ds(pl.multiple_of(c * (group * BLK), 128), group * BLK)
        grid = jnp.dot(coef, table[:, cols], preferred_element_type=jnp.float32)
        for jj in range(JJ):
            for g in range(group):
                pool[jj * XB + c * group + g] = grid[
                    jj * KP : (jj + 1) * KP, g * BLK : (g + 1) * BLK
                ]
        return 0

    lax.fori_loop(0, XB // group, synth, 0)
    half = 2 * BLK
    cells = lax.broadcasted_iota(jnp.int32, (half, BLK), 0).astype(jnp.bfloat16)
    zero = jnp.zeros((half, BLK), jnp.bfloat16)

    first = (lax.axis_index("band") - 1) * (2 * XB)

    def read(b):
        idx = idx_ref[b]
        wgt = wgt_ref[b].astype(jnp.bfloat16)
        total = None
        for h in range(2):
            spot = (idx - h * half).astype(jnp.float32).astype(jnp.bfloat16)
            spread = zero
            for t in range(TAPS):
                hit = cells == jnp.broadcast_to(spot[t : t + 1, :], (half, BLK))
                spread = spread + jnp.where(
                    hit, jnp.broadcast_to(wgt[t : t + 1, :], (half, BLK)), zero
                )
            source = jnp.concatenate(
                [pool[src_ref[2 * h, b] - first], pool[src_ref[2 * h + 1, b] - first]], axis=1
            ).astype(jnp.bfloat16)
            part = jnp.dot(source, spread, preferred_element_type=jnp.float32)
            total = part if total is None else total + part
        return total

    for j in range(2):

        def step(x, _):
            for u in range(8):
                xb = x * 8 + u
                out_ref[:, j, pl.ds(pl.multiple_of(xb * BLK, 128), BLK)] = read(j * XB + xb)[
                    :lev_dev
                ]
            return 0

        lax.fori_loop(0, XB // 8, step, 0)


def grid_part(src, coef, wave, idx, wgt, nb, lev_dev):
    vmem = pl.BlockSpec(memory_space=pltpu.VMEM)
    return pl.pallas_call(
        functools.partial(grid_kernel, nb, lev_dev),
        out_shape=jax.ShapeDtypeStruct((lev_dev, 2, NLON), jnp.float32),
        in_specs=[pl.BlockSpec(memory_space=pltpu.SMEM)] + [vmem] * 4,
        out_specs=vmem,
        scratch_shapes=[
            pltpu.VMEM((nb * RS, NLON), jnp.bfloat16),
            pltpu.VMEM((JJ * XB, KP, BLK), jnp.float32),
        ],
        compiler_params=pltpu.CompilerParams(vmem_limit_bytes=58720256),
    )(src, coef, wave, idx, wgt)


def waves(m_order, nb, slots):
    orders = m_order.astype(jnp.float32).reshape(nb, slots)
    orders = jnp.pad(orders, ((0, 0), (0, SP - slots)), constant_values=-1.0)
    return orders.reshape(nb * SP, 1)


def shards(
    temp_spectrum,
    surf_spectrum,
    legendre,
    m_order,
    hydro_matrix,
    surf_coupling,
    src_blocks,
    tap_index,
    tap_weight,
):
    slots, n_count, _, lev_dev = temp_spectrum.shape
    lat_all = legendre.shape[1]
    nb, nl = lax.axis_size("band"), lax.axis_size("lev")
    band = lax.axis_index("band")
    my_orders = lax.dynamic_slice_in_dim(m_order, band * slots, slots)
    n_index = jnp.arange(n_count, dtype=jnp.int32)
    keep = n_index[None, None, :] >= my_orders[:, None, None]
    values = jnp.where(keep, legendre, jnp.zeros_like(legendre))
    four_t = jnp.einsum(
        "sjn,snrk->sjrk", values, temp_spectrum, preferred_element_type=jnp.float32
    ).astype(jnp.bfloat16)
    four_p = jnp.einsum(
        "sjn,snr->sjr", values, surf_spectrum, preferred_element_type=jnp.float32
    ).astype(jnp.bfloat16)
    four = jnp.concatenate([four_t, four_p[..., None]], axis=3)
    four = jnp.transpose(four, (3, 1, 2, 0))
    four = jnp.pad(four, ((0, LR - lev_dev - 1), (0, 0), (0, 0), (0, SP - slots)))
    four = four.reshape(LR, lat_all * RS)

    coef = exchange(four, hydro_matrix, surf_coupling[None, :], nb, nl)
    out = grid_part(
        src_blocks.T, coef, waves(m_order, nb, slots), tap_index, tap_weight, nb, lev_dev
    )
    return jnp.transpose(out, (1, 0, 2))


def solution(mesh):
    in_specs = (
        P("band", None, None, "lev"),
        P("band", None, None),
        P("band", None, None),
        P(),
        P("lev", None),
        P("lev"),
        P("band", None),
        P("band", None, None),
        P("band", None, None),
    )
    out_specs = P("band", "lev", None)
    return jax.shard_map(shards, mesh=mesh, in_specs=in_specs, out_specs=out_specs, check_vma=False)
```
